32 devices in a mesh: wave: 8 (over z, x), lev: 4 (over y, core).
Axes of the slice: x: 2, y: 2, z: 4, core: 2. Of those that a mesh axis runs over, the one named last changes fastest.
Arguments:
- legendre_values: bfloat16 [1280, 64, 1280], P(('wave', 'lev')), may hold values from -0.15625 to 0.15625
- spectra: bfloat16 [1280, 1280, 128], P(('wave', 'lev')), may hold values from -0.16699219 to 0.16699219
- wave_table: int32 [1280], replicated, may hold values from 0 to 1279, each once
- row_longitudes: int32 [64], P(('wave', 'lev')), may hold values from 20 to 5136, as said below
Outputs:
- grid_fields: float32 [64, 64, 5376], P(('wave', 'lev'))
The draws below stay inside these ranges and needn't reach their ends.
Inputs may be any that keep to these rules, and one draw needn't show every extreme that they name: `wave_table`: every wavenumber appears in exactly one slot. `row_longitudes`: each count is 20 plus a multiple of 4; some row of every draw has 5136.
All inputs are finite; a program needn't handle non-finite values.
Results may differ from the reference program's by a relative error of at most 0.0003.
Values sent between devices are 32-bit elements; how exact they have to be, the bound alone decides.
No kernel may reach another device: no remote copies, remote signals or barrier semaphores. Data moves between devices by JAX's collectives and lax.ppermute only.
A program may use at most 128 MiB of HBM per device.

```python
import jax
import jax.numpy as jnp
from jax import lax

M = 1280
CH = 128
NLAT = 64
NLON = 5376


def draw_row_longitudes(key, part):
    first_key, second_key = jax.random.split(jax.random.fold_in(key, 17))
    steps_drawn = jax.random.randint(first_key, (NLAT,), 0, M)
    chosen_row = jax.random.randint(second_key, (), 0, NLAT)
    steps_drawn = jnp.where(jnp.arange(NLAT) == chosen_row, M - 1, steps_drawn)
    return (20 + 4 * steps_drawn).astype(jnp.int32)


def levels(rng, extent, cuts, smallest, largest):
    def one(position, shards_of):
        draws = jax.random.uniform(jax.random.fold_in(jax.random.fold_in(rng, 6), position), (shards_of,), jnp.float32, smallest / len(cuts), largest / len(cuts))
        return jnp.repeat(jnp.exp(draws), extent[position] // shards_of).reshape((-1,) + (1,) * (len(extent) - position - 1))

    gain = one(*cuts[0])
    for cut in cuts[1:]:
        gain = gain * one(*cut)
    return gain


def normal_values(stream_key, dims, spread, reach, shards=(), kind=jnp.bfloat16):
    loudness = levels(stream_key, dims, shards, -0.22, 0.18) if shards else 1.0
    entries = jax.random.normal(stream_key, dims, jnp.float32) * spread * loudness
    return jnp.minimum(jnp.maximum(entries, -reach), reach).astype(kind)


def setup_inputs(seed: int = 0) -> dict:
    seeds = jax.random.split(jax.random.key(seed), 5)
    return {
        "legendre_values": normal_values(seeds[0], (M, NLAT, M), M ** -0.5, 0.15625, ((0, 32),)),
        "spectra": normal_values(seeds[1], (M, M, CH), (1.0 / M ** 0.5), 0.16699219, ((0, 32),)),
        "wave_table": jax.random.permutation(seeds[2], M).astype(jnp.int32),
        "row_longitudes": draw_row_longitudes(jax.random.fold_in(seeds[4], 71), 0),
    }


def reference(legendre_values, spectra, wave_table, row_longitudes):
    degrees = jnp.arange(M, dtype=jnp.int32)

    def legendre_one(items):
        values, coefficients, wavenumber = items
        kept = jnp.where((degrees >= wavenumber)[:, None], coefficients, jnp.zeros_like(coefficients))
        return jnp.dot(values, kept, preferred_element_type=jnp.float32)

    fourier = lax.map(legendre_one, (legendre_values, spectra, wave_table))
    columns = jnp.arange(NLON, dtype=jnp.int32)
    base_weight = jnp.where(wave_table == 0, jnp.float32(1.0), jnp.float32(2.0))

    def row_one(items):
        coefficients, longitudes = items
        pairs = coefficients.astype(jnp.float32).reshape(M, CH // 2, 2)
        weight = jnp.where(wave_table <= (longitudes - 1) // 2, base_weight, jnp.float32(0.0))
        real_part = pairs[:, :, 0] * weight[:, None]
        imag_part = pairs[:, :, 1] * weight[:, None]
        phase = (wave_table[:, None] * columns[None, :]) % longitudes
        angle = phase.astype(jnp.float32) * (jnp.float32(2.0 * jnp.pi) / longitudes.astype(jnp.float32))
        values = jnp.dot(real_part.T, jnp.cos(angle), precision=lax.Precision.HIGHEST)
        values = values - jnp.dot(imag_part.T, jnp.sin(angle), precision=lax.Precision.HIGHEST)
        return jnp.where(columns[None, :] < longitudes, values, jnp.float32(0.0))

    return lax.map(row_one, (jnp.swapaxes(fourier, 0, 1), row_longitudes))
```

```python
import jax
import jax.numpy as jnp
import numpy as np
from jax import lax
from jax.experimental import pallas as pl
from jax.experimental.pallas import tpu as pltpu
from jax.sharding import PartitionSpec as P

NLON = 5376
HALF = 256
SPAN = 2 * HALF
BLOCKS = -(-NLON // SPAN)
BLOCK_ROWS = 16
TILE = 256
MB = 1 << 20


def fit_turns(function, odd):
    grid = np.cos(np.pi * (np.arange(4000) + 0.5) / 4000) * 0.13 + 0.1301
    roots = np.sqrt(grid)
    values = function(2 * np.pi * roots)
    if odd:
        values = values / roots
    fitted = np.polynomial.chebyshev.Chebyshev.fit(grid, values, 7)
    return [float(c) for c in fitted.convert(kind=np.polynomial.Polynomial).coef]


COS_TERMS = fit_turns(np.cos, False)
SIN_TERMS = fit_turns(np.sin, True)


def horner(terms, square):
    total = jnp.full_like(square, terms[-1])
    for term in terms[-2::-1]:
        total = total * square + term
    return total


def cos_sin(product, double_length, inverse):
    whole = jnp.floor(product * inverse + 0.5)
    turns = (product - whole * double_length) * inverse
    square = turns * turns
    return horner(COS_TERMS, square), horner(SIN_TERMS, square) * turns


def split(values):
    high = values.astype(jnp.bfloat16)
    low = (values - high.astype(jnp.float32)).astype(jnp.bfloat16)
    return high, low


def legendre_kernel(group, slots, wave_ref, legendre_ref, spectra_ref, out_ref):
    step = pl.program_id(0)
    block_number = lax.axis_index("wave") * lax.axis_size("lev") + lax.axis_index("lev")
    degree_count = spectra_ref.shape[1]
    latitudes = legendre_ref.shape[1]

    for index in range(group):
        slot = step * group + index
        wave = wave_ref[block_number * slots + slot]

        def from_tile(tile):
            def branch():
                first = tile * TILE
                degrees = lax.broadcasted_iota(jnp.int32, (latitudes, TILE), 1) + first
                edge = legendre_ref[index, :, first : first + TILE].astype(jnp.float32)
                edge = jnp.where(degrees >= wave, edge, 0.0).astype(jnp.bfloat16)
                total = jnp.dot(
                    edge, spectra_ref[index, first : first + TILE, :], preferred_element_type=jnp.float32
                )
                if first + TILE < degree_count:
                    total = total + jnp.dot(
                        legendre_ref[index, :, first + TILE :],
                        spectra_ref[index, first + TILE :, :],
                        preferred_element_type=jnp.float32,
                    )
                out_ref[pl.ds(slot, latitudes, stride=slots), :] = total

            return branch

        lax.switch(wave // TILE, [from_tile(tile) for tile in range(degree_count // TILE)])


def legendre_stage(legendre_values, spectra, wave_table):
    slots, latitudes, degree_count = legendre_values.shape
    channels = spectra.shape[2]
    group = 8 if slots % 8 == 0 else 1
    return pl.pallas_call(
        lambda *refs: legendre_kernel(group, slots, *refs),
        grid=(slots // group,),
        in_specs=[
            pl.BlockSpec(memory_space=pltpu.SMEM),
            pl.BlockSpec((group, latitudes, degree_count), lambda i: (i, 0, 0)),
            pl.BlockSpec((group, degree_count, channels), lambda i: (i, 0, 0)),
        ],
        out_specs=pl.BlockSpec((latitudes * slots, channels), lambda i: (0, 0)),
        out_shape=jax.ShapeDtypeStruct((latitudes * slots, channels), jnp.float32),
        compiler_params=pltpu.CompilerParams(vmem_limit_bytes=32 * MB),
        name="legendre",
    )(wave_table, legendre_values, spectra)


def table_kernel(length_ref, inverse_ref, lane_waves_ref, row_waves_ref, table_ref, turn_ref):
    row = pl.program_id(0)
    length = length_ref[row]
    inverse = inverse_ref[row]
    double_length = (2 * length).astype(jnp.float32)
    total_waves = row_waves_ref.shape[0]
    chunk = 64

    def fill(step, carry):
        first = pl.multiple_of(step * chunk, chunk)
        waves = row_waves_ref[pl.ds(first, chunk), :]
        for part in range(HALF // 128):
            lanes = lax.broadcasted_iota(jnp.int32, (chunk, 128), 1) + part * 128
            offsets = (2 * lanes + 1).astype(jnp.float32)
            values = cos_sin(waves * offsets, double_length, inverse)
            for kind in range(2):
                high, low = split(values[kind])
                table_ref[0, kind, 0, pl.ds(first, chunk), pl.ds(part * 128, 128)] = high
                table_ref[0, kind, 1, pl.ds(first, chunk), pl.ds(part * 128, 128)] = low
        return carry

    lax.fori_loop(0, total_waves // chunk, fill, 0)
    blocks = lax.broadcasted_iota(jnp.int32, (BLOCK_ROWS, total_waves), 0)
    centres = (2 * SPAN * blocks + (SPAN - 1)).astype(jnp.float32)
    waves = lane_waves_ref[0:1, :]
    turn_cos, turn_sin = cos_sin(waves * centres, double_length, inverse)
    limit = lax.shift_right_logical(length - 1, 1).astype(jnp.float32)
    weight = jnp.where(waves > limit, 0.0, jnp.where(waves == 0.0, 1.0, 2.0))
    turn_ref[0, 0] = turn_cos * weight
    turn_ref[0, 1] = turn_sin * weight


def table_stage(wave_table, row_longitudes):
    total_waves = wave_table.shape[0]
    local_rows = row_longitudes.shape[0]
    waves = wave_table.astype(jnp.float32)
    lane_waves = jnp.broadcast_to(waves[None, :], (8, total_waves))
    row_waves = jnp.broadcast_to(waves[:, None], (total_waves, 128))
    inverse = 0.5 / row_longitudes.astype(jnp.float32)
    entries = local_rows * total_waves * HALF
    return pl.pallas_call(
        table_kernel,
        grid=(local_rows,),
        in_specs=[
            pl.BlockSpec(memory_space=pltpu.SMEM),
            pl.BlockSpec(memory_space=pltpu.SMEM),
            pl.BlockSpec((8, total_waves), lambda i: (0, 0)),
            pl.BlockSpec((total_waves, 128), lambda i: (0, 0)),
        ],
        out_specs=[
            pl.BlockSpec((1, 2, 2, total_waves, HALF), lambda i: (i, 0, 0, 0, 0)),
            pl.BlockSpec((1, 2, BLOCK_ROWS, total_waves), lambda i: (i, 0, 0, 0)),
        ],
        out_shape=[
            jax.ShapeDtypeStruct((local_rows, 2, 2, total_waves, HALF), jnp.bfloat16),
            jax.ShapeDtypeStruct((local_rows, 2, BLOCK_ROWS, total_waves), jnp.float32),
        ],
        compiler_params=pltpu.CompilerParams(vmem_limit_bytes=32 * MB),
        cost_estimate=pl.CostEstimate(flops=entries * 40, bytes_accessed=entries * 8, transcendentals=0),
        name="trig_tables",
    )(row_longitudes, inverse, lane_waves, row_waves)


def fourier_kernel(length_ref, moved_ref, table_ref, turn_ref, out_ref, flipped_ref, real_ref, imag_ref):
    row = pl.program_id(0)
    senders, _, slots, channels = moved_ref.shape
    total_waves = senders * slots
    fields = channels // 2
    length = length_ref[row]

    moved = moved_ref[...].reshape(total_waves, channels)
    for step in range(total_waves // 128):
        lanes = slice(step * 128, (step + 1) * 128)
        flipped_ref[step] = moved[lanes].T
        real_ref[:, lanes] = flipped_ref[step, pl.ds(0, fields, stride=2), :]
        imag_ref[:, lanes] = flipped_ref[step, pl.ds(1, fields, stride=2), :]
    out_ref[...] = jnp.zeros_like(out_ref)
    reverse = 127 - lax.broadcasted_iota(jnp.int32, (fields, 128), 1)

    def one_block(block, carry):
        totals = [jnp.zeros((fields, HALF), jnp.float32) for _ in range(2)]
        for tile in range(total_waves // TILE):
            lanes = pl.ds(tile * TILE, TILE)
            real = real_ref[:, lanes]
            imag = imag_ref[:, lanes]
            turn_cos = turn_ref[0, 0, pl.ds(block, 1), lanes]
            turn_sin = turn_ref[0, 1, pl.ds(block, 1), lanes]
            sides = (real * turn_cos - imag * turn_sin, real * turn_sin + imag * turn_cos)
            for kind in range(2):
                high, low = split(sides[kind])
                both = jnp.concatenate([high, low], axis=0)
                piece = jnp.dot(both, table_ref[0, kind, 0, lanes, :], preferred_element_type=jnp.float32)
                rest = jnp.dot(high, table_ref[0, kind, 1, lanes, :], preferred_element_type=jnp.float32)
                totals[kind] = totals[kind] + (piece[:fields] + piece[fields:] + rest)
        even, odd = totals
        first = pl.multiple_of(block * SPAN, SPAN)
        below = even + odd
        parts = [below[:, p * 128 : (p + 1) * 128] for p in range(HALF // 128)]
        parts = [jnp.take_along_axis(part, reverse, axis=1) for part in parts[::-1]]
        below = jnp.concatenate(parts, axis=1)
        columns = lax.broadcasted_iota(jnp.int32, (fields, HALF), 1) + first
        out_ref[0, :, pl.ds(first, HALF)] = jnp.where(columns < length, below, 0.0)

        @pl.when(first + HALF < NLON)
        def _():
            later = pl.multiple_of(first + HALF, HALF)
            above = even - odd
            out_ref[0, :, pl.ds(later, HALF)] = jnp.where(columns + HALF < length, above, 0.0)

        return carry

    lax.fori_loop(0, (length + SPAN - 1) // SPAN, one_block, 0)


def fourier_stage(moved, tables, turns, row_longitudes):
    senders, local_rows, slots, channels = moved.shape
    total_waves = senders * slots
    fields = channels // 2
    return pl.pallas_call(
        fourier_kernel,
        grid=(local_rows,),
        in_specs=[
            pl.BlockSpec(memory_space=pltpu.SMEM),
            pl.BlockSpec((senders, 1, slots, channels), lambda i: (0, i, 0, 0)),
            pl.BlockSpec((1, 2, 2, total_waves, HALF), lambda i: (i, 0, 0, 0, 0)),
            pl.BlockSpec((1, 2, BLOCK_ROWS, total_waves), lambda i: (i, 0, 0, 0)),
        ],
        out_specs=pl.BlockSpec((1, fields, NLON), lambda i: (i, 0, 0)),
        out_shape=jax.ShapeDtypeStruct((local_rows, fields, NLON), jnp.float32),
        scratch_shapes=[
            pltpu.VMEM((total_waves // 128, channels, 128), jnp.float32),
            pltpu.VMEM((fields, total_waves), jnp.float32),
            pltpu.VMEM((fields, total_waves), jnp.float32),
        ],
        compiler_params=pltpu.CompilerParams(vmem_limit_bytes=40 * MB),
        name="fourier",
    )(row_longitudes, moved, tables, turns)


def per_device(legendre_values, spectra, wave_table, row_longitudes):
    slots = legendre_values.shape[0]
    devices = lax.axis_size("wave") * lax.axis_size("lev")
    local_rows = row_longitudes.shape[0]
    total_waves = wave_table.shape[0]
    sent = legendre_stage(legendre_values, spectra, wave_table)
    channels = sent.shape[1]
    moved = lax.all_to_all(
        sent.reshape(devices, local_rows * slots, channels), ("wave", "lev"), split_axis=0, concat_axis=0, tiled=True
    ).reshape(devices, local_rows, slots, channels)
    if slots % 8:
        moved = moved.swapaxes(0, 1).reshape(1, local_rows, devices * slots, channels)
    tables, turns = table_stage(wave_table, row_longitudes)
    return fourier_stage(moved, tables, turns, row_longitudes)


def solution(mesh):
    in_specs = (
        P(("wave", "lev"), None, None),
        P(("wave", "lev"), None, None),
        P(),
        P(("wave", "lev")),
    )
    out_specs = P(("wave", "lev"), None, None)
    return jax.shard_map(
        per_device, mesh=mesh, in_specs=in_specs, out_specs=out_specs, check_vma=False
    )
```

```python
import jax
import jax.numpy as jnp
import numpy as np
from jax import lax
from jax.experimental import pallas as pl
from jax.experimental.pallas import tpu as pltpu
from jax.sharding import PartitionSpec as P

NLON = 5376
HALF = 256
SPAN = 2 * HALF
BLOCKS = -(-NLON // SPAN)
BLOCK_ROWS = 16
WHOLE = NLON // SPAN
SKIP = 16
PART = 8
GROUP = 5
TILE = 256
MB = 1 << 20


def fit_turns(function, odd):
    grid = np.cos(np.pi * (np.arange(4000) + 0.5) / 4000) * 0.13 + 0.1301
    roots = np.sqrt(grid)
    values = function(2 * np.pi * roots)
    if odd:
        values = values / roots
    fitted = np.polynomial.chebyshev.Chebyshev.fit(grid, values, 7)
    return [float(c) for c in fitted.convert(kind=np.polynomial.Polynomial).coef]


COS_TERMS = fit_turns(np.cos, False)
SIN_TERMS = fit_turns(np.sin, True)


def horner(terms, square):
    total = jnp.full_like(square, terms[-1])
    for term in terms[-2::-1]:
        total = total * square + term
    return total


def cos_sin(product, double_length, inverse):
    whole = jnp.floor(product * inverse + 0.5)
    turns = (product - whole * double_length) * inverse
    square = turns * turns
    return horner(COS_TERMS, square), horner(SIN_TERMS, square) * turns


def split(values):
    high = values.astype(jnp.bfloat16)
    low = (values - high.astype(jnp.float32)).astype(jnp.bfloat16)
    return high, low


def legendre_kernel(
    group, wave_in_ref, legendre_ref, spectra_ref, out_ref, wave_ref, values_ref, kept_ref, sums_ref,
    wave_sem, value_sems, in_sems, out_sems,
):
    slots, latitudes, degree_count = legendre_ref.shape
    block_number = lax.axis_index("wave") * lax.axis_size("lev") + lax.axis_index("lev")
    first_slot = block_number * slots
    wave_fetch = pltpu.make_async_copy(wave_in_ref, wave_ref, wave_sem)
    wave_fetch.start()

    def fetch(slot):
        first = pl.multiple_of(wave_ref[first_slot + slot] // SKIP * SKIP, SKIP)
        rows = pl.ds(first, degree_count - first)
        return (
            pltpu.make_async_copy(spectra_ref.at[slot, rows, :], kept_ref.at[slot, rows, :], in_sems.at[slot]),
        )

    def fetch_values(step):
        part = pl.ds(pl.multiple_of(step * group, group), group)
        return pltpu.make_async_copy(legendre_ref.at[part], values_ref.at[part], value_sems.at[step])

    def start_slot(slot, carry):
        for copy in fetch(slot):
            copy.start()
        return carry

    def send(step):
        first = pl.multiple_of(step * group, group)
        return pltpu.make_async_copy(sums_ref.at[step], out_ref.at[:, pl.ds(first, group), :], out_sems.at[step])

    degrees = lax.broadcasted_iota(jnp.int16, kept_ref.shape[1:], 0)

    def group_sums(step, carry):
        for first in range(0, group, PART):
            part = range(first, min(first + PART, group))
            if first == 0:
                fetch_values(step).wait()
            for index in part:
                for copy in fetch(step * group + index):
                    copy.wait()
            for index in part:
                slot = step * group + index
                wave = wave_ref[first_slot + slot]
                kept = jnp.where(degrees >= wave.astype(jnp.int16), kept_ref[slot], jnp.bfloat16(0))
                sums_ref[step, :, index, :] = jnp.dot(
                    values_ref[slot], kept, preferred_element_type=jnp.float32
                )
        send(step).start()
        return carry

    def finish_send(step, carry):
        send(step).wait()
        return carry

    fetch_values(0).start()
    wave_fetch.wait()
    for step in range(slots // group):
        if step:
            fetch_values(step).start()
        lax.fori_loop(step * group, step * group + group, start_slot, 0)
    lax.fori_loop(0, slots // group, group_sums, 0)
    lax.fori_loop(0, slots // group, finish_send, 0)


def legendre_stage(legendre_values, spectra, wave_table):
    slots, latitudes, degree_count = legendre_values.shape
    channels = spectra.shape[2]
    group = 8 if slots % 8 == 0 else slots
    return pl.pallas_call(
        lambda *refs: legendre_kernel(group, *refs),
        in_specs=[pl.BlockSpec(memory_space=pltpu.HBM)] * 3,
        out_specs=pl.BlockSpec(memory_space=pltpu.HBM),
        out_shape=jax.ShapeDtypeStruct((latitudes, slots, channels), jnp.float32),
        scratch_shapes=[
            pltpu.SMEM(wave_table.shape, wave_table.dtype),
            pltpu.VMEM((slots, latitudes, degree_count), jnp.bfloat16),
            pltpu.VMEM((slots, degree_count, channels), jnp.bfloat16),
            pltpu.VMEM((slots // group, latitudes, group, channels), jnp.float32),
            pltpu.SemaphoreType.DMA,
            pltpu.SemaphoreType.DMA((slots // group,)),
            pltpu.SemaphoreType.DMA((slots,)),
            pltpu.SemaphoreType.DMA((slots // group,)),
        ],
        compiler_params=pltpu.CompilerParams(vmem_limit_bytes=60 * MB),
        name="legendre",
    )(wave_table, legendre_values, spectra)


def table_kernel(length_ref, inverse_ref, lane_waves_ref, row_waves_ref, table_ref, turn_ref):
    row = pl.program_id(0)
    length = length_ref[row]
    inverse = inverse_ref[row]
    double_length = (2 * length).astype(jnp.float32)
    total_waves = row_waves_ref.shape[0]
    chunk = 64

    def fill(step, carry):
        first = pl.multiple_of(step * chunk, chunk)
        waves = row_waves_ref[pl.ds(first, chunk), :]
        for part in range(HALF // 128):
            lanes = lax.broadcasted_iota(jnp.int32, (chunk, 128), 1) + part * 128
            offsets = (2 * lanes + 1).astype(jnp.float32)
            values = cos_sin(waves * offsets, double_length, inverse)
            for kind in range(2):
                high, low = split(values[kind])
                table_ref[0, kind, 0, pl.ds(first, chunk), pl.ds(part * 128, 128)] = high
                table_ref[0, kind, 1, pl.ds(first, chunk), pl.ds(part * 128, 128)] = low
        return carry

    lax.fori_loop(0, total_waves // chunk, fill, 0)
    blocks = lax.broadcasted_iota(jnp.int32, (BLOCK_ROWS, total_waves), 0)
    centres = (2 * SPAN * blocks + (SPAN - 1)).astype(jnp.float32)
    waves = lane_waves_ref[0:1, :]
    turn_cos, turn_sin = cos_sin(waves * centres, double_length, inverse)
    limit = lax.shift_right_logical(length - 1, 1).astype(jnp.float32)
    weight = jnp.where(waves > limit, 0.0, jnp.where(waves == 0.0, 1.0, 2.0))
    turn_ref[0, 0] = turn_cos * weight
    turn_ref[0, 1] = turn_sin * weight


def table_stage(wave_table, row_longitudes):
    total_waves = wave_table.shape[0]
    local_rows = row_longitudes.shape[0]
    waves = wave_table.astype(jnp.float32)
    lane_waves = jnp.broadcast_to(waves[None, :], (8, total_waves))
    row_waves = jnp.broadcast_to(waves[:, None], (total_waves, 128))
    inverse = 0.5 / row_longitudes.astype(jnp.float32)
    entries = local_rows * total_waves * HALF
    return pl.pallas_call(
        table_kernel,
        grid=(local_rows,),
        in_specs=[
            pl.BlockSpec(memory_space=pltpu.SMEM),
            pl.BlockSpec(memory_space=pltpu.SMEM),
            pl.BlockSpec((8, total_waves), lambda i: (0, 0)),
            pl.BlockSpec((total_waves, 128), lambda i: (0, 0)),
        ],
        out_specs=[
            pl.BlockSpec((1, 2, 2, total_waves, HALF), lambda i: (i, 0, 0, 0, 0)),
            pl.BlockSpec((1, 2, BLOCK_ROWS, total_waves), lambda i: (i, 0, 0, 0)),
        ],
        out_shape=[
            pltpu.HBM((local_rows, 2, 2, total_waves, HALF), jnp.bfloat16),
            pltpu.HBM((local_rows, 2, BLOCK_ROWS, total_waves), jnp.float32),
        ],
        compiler_params=pltpu.CompilerParams(vmem_limit_bytes=32 * MB),
        cost_estimate=pl.CostEstimate(flops=entries * 40, bytes_accessed=entries * 8, transcendentals=0),
        name="trig_tables",
    )(row_longitudes, inverse, lane_waves, row_waves)


def fourier_kernel(
    length_in_ref, moved_in_ref, table_in_ref, turn_in_ref, out_ref,
    length_ref, moved_ref, table_ref, turn_ref, flipped_ref, real_ref, imag_ref, side_ref, result_ref,
    length_sem, in_sems, out_sems,
):
    senders, local_rows, slots, channels = moved_ref.shape
    total_waves = senders * slots
    fields = channels // 2
    length_fetch = pltpu.make_async_copy(length_in_ref, length_ref, length_sem)
    fetch_moved, fetch_turns, fetch_table = [], [], []
    for row in range(local_rows):
        fetch_moved.append(pltpu.make_async_copy(moved_in_ref.at[:, row], moved_ref.at[:, row], in_sems.at[row, 0]))
        fetch_turns.append(pltpu.make_async_copy(turn_in_ref.at[row], turn_ref.at[row], in_sems.at[row, 1]))
        fetch_table.append(pltpu.make_async_copy(table_in_ref.at[row], table_ref.at[row], in_sems.at[row, 2]))
    length_fetch.start()

    for row in range(local_rows):
        fetch_moved[row].start()

    def fetch_row(row):
        fetch_turns[row].start()
        fetch_table[row].start()

    fetch_row(0)

    def send(row, block):
        columns = pl.ds(pl.multiple_of(block * SPAN, SPAN), SPAN)
        return pltpu.make_async_copy(
            result_ref.at[row, :, columns], out_ref.at[row, :, columns], out_sems.at[row, block]
        )

    def send_last(row):
        columns = pl.ds(WHOLE * SPAN, NLON - WHOLE * SPAN)
        return pltpu.make_async_copy(
            result_ref.at[row, :, columns], out_ref.at[row, :, columns], out_sems.at[row, WHOLE]
        )

    def turn_row(row):
        moved = moved_ref[:, row].reshape(total_waves, channels)
        for step in range(total_waves // 128):
            lanes = slice(step * 128, (step + 1) * 128)
            flipped_ref[step] = moved[lanes].T
            real_ref[row, :, lanes] = flipped_ref[step, pl.ds(0, fields, stride=2), :]
            imag_ref[row, :, lanes] = flipped_ref[step, pl.ds(1, fields, stride=2), :]

    result_ref[...] = jnp.zeros_like(result_ref)
    reverse = 127 - lax.broadcasted_iota(jnp.int32, (fields, 128), 1)

    def rotate(row, first_block, count):
        for tile in range(total_waves // TILE):
            lanes = slice(tile * TILE, (tile + 1) * TILE)
            real = real_ref[row, :, lanes]
            imag = imag_ref[row, :, lanes]
            for index in range(count):
                turn_cos = turn_ref[row, 0, pl.ds(first_block + index, 1), lanes]
                turn_sin = turn_ref[row, 1, pl.ds(first_block + index, 1), lanes]
                sides = (real * turn_cos - imag * turn_sin, real * turn_sin + imag * turn_cos)
                for kind in range(2):
                    high, low = split(sides[kind])
                    side_ref[kind, index * fields : (index + 1) * fields, lanes] = high
                    side_ref[kind, (count + index) * fields : (count + index + 1) * fields, lanes] = low

    def transform(row, length, first_block, count):
        high_rows = count * fields
        sums = []
        for kind in range(2):
            piece = jnp.dot(
                side_ref[kind, : 2 * high_rows], table_ref[row, kind, 0], preferred_element_type=jnp.float32
            )
            rest = jnp.dot(side_ref[kind, :high_rows], table_ref[row, kind, 1], preferred_element_type=jnp.float32)
            sums.append(piece[:high_rows] + piece[high_rows:] + rest)
        for index in range(count):
            block = first_block + index
            even = sums[0][index * fields : (index + 1) * fields]
            odd = sums[1][index * fields : (index + 1) * fields]
            first = pl.multiple_of(block * SPAN, SPAN)
            below = even + odd
            parts = [below[:, p * 128 : (p + 1) * 128] for p in range(HALF // 128)]
            parts = [jnp.take_along_axis(part, reverse, axis=1) for part in parts[::-1]]
            below = jnp.concatenate(parts, axis=1)
            columns = lax.broadcasted_iota(jnp.int32, (fields, HALF), 1) + first
            result_ref[row, :, pl.ds(first, HALF)] = jnp.where(columns < length, below, 0.0)
            later = pl.multiple_of(first + HALF, HALF)
            result_ref[row, :, pl.ds(later, HALF)] = jnp.where(columns + HALF < length, even - odd, 0.0)

            @pl.when(block < WHOLE)
            def _():
                send(row, block).start()

    length_fetch.wait()
    for row in range(local_rows):
        length = length_ref[row]
        block_count = (length + SPAN - 1) // SPAN
        tail = lax.rem(block_count, GROUP) == 1
        group_count = jnp.where(tail, block_count // GROUP, (block_count + GROUP - 1) // GROUP)
        filled = jnp.minimum(group_count * GROUP + tail.astype(jnp.int32), WHOLE)

        def send_empty(block, carry):
            send(row, block).start()
            return carry

        lax.fori_loop(filled, WHOLE, send_empty, 0)
        if row == 0:
            for each in range(local_rows):
                fetch_moved[each].wait()
                turn_row(each)
        fetch_turns[row].wait()
        fetch_table[row].wait()
        if row + 1 < local_rows:
            fetch_row(row + 1)

        def one_group(group, carry):
            rotate(row, group * GROUP, GROUP)

            transform(row, length, group * GROUP, GROUP)
            return carry

        lax.fori_loop(0, group_count, one_group, 0)

        @pl.when(tail)
        def _():
            rotate(row, group_count * GROUP, 1)

            transform(row, length, group_count * GROUP, 1)

        send_last(row).start()

    for row in range(local_rows):
        for block in range(WHOLE):
            send(row, block).wait()
        send_last(row).wait()


def fourier_stage(moved, tables, turns, row_longitudes):
    senders, local_rows, slots, channels = moved.shape
    total_waves = senders * slots
    fields = channels // 2
    return pl.pallas_call(
        fourier_kernel,
        in_specs=[
            pl.BlockSpec(memory_space=pl.ANY),
            pl.BlockSpec(memory_space=pl.ANY),
            pl.BlockSpec(memory_space=pltpu.HBM),
            pl.BlockSpec(memory_space=pltpu.HBM),
        ],
        out_specs=pl.BlockSpec(memory_space=pltpu.HBM),
        out_shape=jax.ShapeDtypeStruct((local_rows, fields, NLON), jnp.float32),
        scratch_shapes=[
            pltpu.SMEM(row_longitudes.shape, row_longitudes.dtype),
            pltpu.VMEM(moved.shape, moved.dtype),
            pltpu.VMEM(tables.shape, tables.dtype),
            pltpu.VMEM(turns.shape, turns.dtype),
            pltpu.VMEM((total_waves // 128, channels, 128), jnp.float32),
            pltpu.VMEM((local_rows, fields, total_waves), jnp.float32),
            pltpu.VMEM((local_rows, fields, total_waves), jnp.float32),
            pltpu.VMEM((2, 2 * GROUP * fields, total_waves), jnp.bfloat16),
            pltpu.VMEM((local_rows, fields, (BLOCKS + GROUP) * SPAN), jnp.float32),
            pltpu.SemaphoreType.DMA,
            pltpu.SemaphoreType.DMA((local_rows, 3)),
            pltpu.SemaphoreType.DMA((local_rows, BLOCKS)),
        ],
        compiler_params=pltpu.CompilerParams(vmem_limit_bytes=50 * MB),
        name="fourier",
    )(row_longitudes, moved, tables, turns)


def per_device(legendre_values, spectra, wave_table, row_longitudes):
    slots = legendre_values.shape[0]
    devices = lax.axis_size("wave") * lax.axis_size("lev")
    local_rows = row_longitudes.shape[0]
    total_waves = wave_table.shape[0]
    sent = legendre_stage(legendre_values, spectra, wave_table)
    channels = sent.shape[2]
    moved = lax.all_to_all(
        sent.reshape(devices, local_rows * slots, channels), ("wave", "lev"), split_axis=0, concat_axis=0, tiled=True
    ).reshape(devices, local_rows, slots, channels)
    if slots % 8:
        moved = moved.swapaxes(0, 1).reshape(1, local_rows, devices * slots, channels)
    tables, turns = table_stage(wave_table, row_longitudes)
    return fourier_stage(moved, tables, turns, row_longitudes)


def solution(mesh):
    in_specs = (
        P(("wave", "lev"), None, None),
        P(("wave", "lev"), None, None),
        P(),
        P(("wave", "lev")),
    )
    out_specs = P(("wave", "lev"), None, None)
    return jax.shard_map(
        per_device, mesh=mesh, in_specs=in_specs, out_specs=out_specs, check_vma=False
    )
```

```python
import jax
import jax.numpy as jnp
import numpy as np
from jax import lax
from jax.experimental import pallas as pl
from jax.experimental.pallas import tpu as pltpu
from jax.sharding import PartitionSpec as P

NLON = 5376
HALF = 256
SPAN = 2 * HALF
BLOCKS = -(-NLON // SPAN)
BLOCK_ROWS = 16
WHOLE = NLON // SPAN
SKIP = 16
PART = 8
GROUP = 5
TILE = 256
MB = 1 << 20


def fit_turns(function, odd):
    grid = np.cos(np.pi * (np.arange(4000) + 0.5) / 4000) * 0.13 + 0.1301
    roots = np.sqrt(grid)
    values = function(2 * np.pi * roots)
    if odd:
        values = values / roots
    fitted = np.polynomial.chebyshev.Chebyshev.fit(grid, values, 7)
    return [float(c) for c in fitted.convert(kind=np.polynomial.Polynomial).coef]


COS_TERMS = fit_turns(np.cos, False)
SIN_TERMS = fit_turns(np.sin, True)


def horner(terms, square):
    total = jnp.full_like(square, terms[-1])
    for term in terms[-2::-1]:
        total = total * square + term
    return total


def cos_sin(product, double_length, inverse):
    whole = jnp.floor(product * inverse + 0.5)
    turns = (product - whole * double_length) * inverse
    square = turns * turns
    return horner(COS_TERMS, square), horner(SIN_TERMS, square) * turns


def split(values):
    high = values.astype(jnp.bfloat16)
    low = (values - high.astype(jnp.float32)).astype(jnp.bfloat16)
    return high, low


def legendre_kernel(
    group, wave_in_ref, legendre_ref, spectra_ref, out_ref, wave_ref, values_ref, kept_ref, sums_ref,
    wave_sem, value_sems, in_sems, out_sems,
):
    slots, latitudes, degree_count = legendre_ref.shape
    block_number = lax.axis_index("wave") * lax.axis_size("lev") + lax.axis_index("lev")
    first_slot = block_number * slots
    wave_fetch = pltpu.make_async_copy(wave_in_ref, wave_ref, wave_sem)
    wave_fetch.start()

    def fetch(slot):
        first = pl.multiple_of(wave_ref[first_slot + slot] // SKIP * SKIP, SKIP)
        rows = pl.ds(first, degree_count - first)
        return (
            pltpu.make_async_copy(spectra_ref.at[slot, rows, :], kept_ref.at[slot, rows, :], in_sems.at[slot]),
        )

    def fetch_values(step):
        part = pl.ds(pl.multiple_of(step * group, group), group)
        return pltpu.make_async_copy(legendre_ref.at[part], values_ref.at[part], value_sems.at[step])

    def start_slot(slot, carry):
        for copy in fetch(slot):
            copy.start()
        return carry

    def send(step):
        first = pl.multiple_of(step * group, group)
        return pltpu.make_async_copy(sums_ref.at[step], out_ref.at[:, pl.ds(first, group), :], out_sems.at[step])

    degrees = lax.broadcasted_iota(jnp.int16, kept_ref.shape[1:], 0)

    def group_sums(step, carry):
        for first in range(0, group, PART):
            part = range(first, min(first + PART, group))
            if first == 0:
                fetch_values(step).wait()
            for index in part:
                for copy in fetch(step * group + index):
                    copy.wait()
            for index in part:
                slot = step * group + index
                wave = wave_ref[first_slot + slot]
                kept = jnp.where(degrees >= wave.astype(jnp.int16), kept_ref[slot], jnp.bfloat16(0))
                sums_ref[step, :, index, :] = jnp.dot(
                    values_ref[slot], kept, preferred_element_type=jnp.float32
                )
        send(step).start()
        return carry

    def finish_send(step, carry):
        send(step).wait()
        return carry

    fetch_values(0).start()
    wave_fetch.wait()
    for step in range(slots // group):
        if step:
            fetch_values(step).start()
        lax.fori_loop(step * group, step * group + group, start_slot, 0)
    lax.fori_loop(0, slots // group, group_sums, 0)
    lax.fori_loop(0, slots // group, finish_send, 0)


def legendre_stage(legendre_values, spectra, wave_table):
    slots, latitudes, degree_count = legendre_values.shape
    channels = spectra.shape[2]
    group = 8 if slots % 8 == 0 else slots
    return pl.pallas_call(
        lambda *refs: legendre_kernel(group, *refs),
        in_specs=[pl.BlockSpec(memory_space=pltpu.HBM)] * 3,
        out_specs=pl.BlockSpec(memory_space=pltpu.HBM),
        out_shape=jax.ShapeDtypeStruct((latitudes, slots, channels), jnp.float32),
        scratch_shapes=[
            pltpu.SMEM(wave_table.shape, wave_table.dtype),
            pltpu.VMEM((slots, latitudes, degree_count), jnp.bfloat16),
            pltpu.VMEM((slots, degree_count, channels), jnp.bfloat16),
            pltpu.VMEM((slots // group, latitudes, group, channels), jnp.float32),
            pltpu.SemaphoreType.DMA,
            pltpu.SemaphoreType.DMA((slots // group,)),
            pltpu.SemaphoreType.DMA((slots,)),
            pltpu.SemaphoreType.DMA((slots // group,)),
        ],
        compiler_params=pltpu.CompilerParams(vmem_limit_bytes=60 * MB),
        name="legendre",
    )(wave_table, legendre_values, spectra)


def table_kernel(length_ref, inverse_ref, lane_waves_ref, row_waves_ref, table_ref, turn_ref):
    row = pl.program_id(0)
    length = length_ref[row]
    inverse = inverse_ref[row]
    double_length = (2 * length).astype(jnp.float32)
    total_waves = row_waves_ref.shape[0]
    chunk = 64

    def fill(step, carry):
        first = pl.multiple_of(step * chunk, chunk)
        waves = row_waves_ref[pl.ds(first, chunk), :]
        for part in range(HALF // 128):
            lanes = lax.broadcasted_iota(jnp.int32, (chunk, 128), 1) + part * 128
            offsets = (2 * lanes + 1).astype(jnp.float32)
            values = cos_sin(waves * offsets, double_length, inverse)
            for kind in range(2):
                high, low = split(values[kind])
                table_ref[0, kind, 0, pl.ds(first, chunk), pl.ds(part * 128, 128)] = high
                table_ref[0, kind, 1, pl.ds(first, chunk), pl.ds(part * 128, 128)] = low
        return carry

    lax.fori_loop(0, total_waves // chunk, fill, 0)
    blocks = lax.broadcasted_iota(jnp.int32, (BLOCK_ROWS, total_waves), 0)
    centres = (2 * SPAN * blocks + (SPAN - 1)).astype(jnp.float32)
    waves = lane_waves_ref[0:1, :]
    turn_cos, turn_sin = cos_sin(waves * centres, double_length, inverse)
    limit = lax.shift_right_logical(length - 1, 1).astype(jnp.float32)
    weight = jnp.where(waves > limit, 0.0, jnp.where(waves == 0.0, 1.0, 2.0))
    turn_ref[0, 0] = turn_cos * weight
    turn_ref[0, 1] = turn_sin * weight


def table_stage(wave_table, row_longitudes):
    total_waves = wave_table.shape[0]
    local_rows = row_longitudes.shape[0]
    waves = wave_table.astype(jnp.float32)
    lane_waves = jnp.broadcast_to(waves[None, :], (8, total_waves))
    row_waves = jnp.broadcast_to(waves[:, None], (total_waves, 128))
    inverse = 0.5 / row_longitudes.astype(jnp.float32)
    entries = local_rows * total_waves * HALF
    return pl.pallas_call(
        table_kernel,
        grid=(local_rows,),
        in_specs=[
            pl.BlockSpec(memory_space=pltpu.SMEM),
            pl.BlockSpec(memory_space=pltpu.SMEM),
            pl.BlockSpec((8, total_waves), lambda i: (0, 0)),
            pl.BlockSpec((total_waves, 128), lambda i: (0, 0)),
        ],
        out_specs=[
            pl.BlockSpec((1, 2, 2, total_waves, HALF), lambda i: (i, 0, 0, 0, 0)),
            pl.BlockSpec((1, 2, BLOCK_ROWS, total_waves), lambda i: (i, 0, 0, 0)),
        ],
        out_shape=[
            pltpu.HBM((local_rows, 2, 2, total_waves, HALF), jnp.bfloat16),
            pltpu.HBM((local_rows, 2, BLOCK_ROWS, total_waves), jnp.float32),
        ],
        compiler_params=pltpu.CompilerParams(vmem_limit_bytes=32 * MB),
        cost_estimate=pl.CostEstimate(flops=entries * 40, bytes_accessed=entries * 8, transcendentals=0),
        name="trig_tables",
    )(row_longitudes, inverse, lane_waves, row_waves)


def fourier_kernel(
    length_in_ref, moved_in_ref, table_in_ref, turn_in_ref, out_ref,
    length_ref, moved_ref, table_ref, turn_ref, flipped_ref, real_ref, imag_ref, side_ref, result_ref,
    length_sem, in_sems, out_sems,
):
    senders, local_rows, slots, channels = moved_ref.shape
    total_waves = senders * slots
    fields = channels // 2
    length_fetch = pltpu.make_async_copy(length_in_ref, length_ref, length_sem)
    fetch_moved, fetch_turns, fetch_table = [], [], []
    for row in range(local_rows):
        fetch_moved.append(pltpu.make_async_copy(moved_in_ref.at[:, row], moved_ref.at[:, row], in_sems.at[row, 0]))
        fetch_turns.append(pltpu.make_async_copy(turn_in_ref.at[row], turn_ref.at[row], in_sems.at[row, 1]))
        fetch_table.append(pltpu.make_async_copy(table_in_ref.at[row], table_ref.at[row], in_sems.at[row, 2]))
    length_fetch.start()

    for row in range(local_rows):
        fetch_moved[row].start()

    def fetch_row(row):
        fetch_turns[row].start()
        fetch_table[row].start()

    fetch_row(0)

    def send(row, block):
        columns = pl.ds(pl.multiple_of(block * SPAN, SPAN), SPAN)
        return pltpu.make_async_copy(
            result_ref.at[row, :, columns], out_ref.at[row, :, columns], out_sems.at[row, block]
        )

    def send_last(row):
        columns = pl.ds(WHOLE * SPAN, NLON - WHOLE * SPAN)
        return pltpu.make_async_copy(
            result_ref.at[row, :, columns], out_ref.at[row, :, columns], out_sems.at[row, WHOLE]
        )

    def turn_row(row):
        moved = moved_ref[:, row].reshape(total_waves, channels)
        for step in range(total_waves // 128):
            lanes = slice(step * 128, (step + 1) * 128)
            flipped_ref[step] = moved[lanes].T
            real_ref[row, :, lanes] = flipped_ref[step, pl.ds(0, fields, stride=2), :]
            imag_ref[row, :, lanes] = flipped_ref[step, pl.ds(1, fields, stride=2), :]

    result_ref[...] = jnp.zeros_like(result_ref)
    reverse = 127 - lax.broadcasted_iota(jnp.int32, (fields, 128), 1)

    def rotate(row, first_block, count):
        for tile in range(total_waves // TILE):
            lanes = slice(tile * TILE, (tile + 1) * TILE)
            real = real_ref[row, :, lanes]
            imag = imag_ref[row, :, lanes]
            for index in range(count):
                turn_cos = turn_ref[row, 0, pl.ds(first_block + index, 1), lanes]
                turn_sin = turn_ref[row, 1, pl.ds(first_block + index, 1), lanes]
                sides = (real * turn_cos - imag * turn_sin, real * turn_sin + imag * turn_cos)
                for kind in range(2):
                    high, low = split(sides[kind])
                    side_ref[kind, index * fields : (index + 1) * fields, lanes] = high
                    side_ref[kind, (count + index) * fields : (count + index + 1) * fields, lanes] = low

    def transform(row, length, first_block, count):
        high_rows = count * fields
        sums = []
        for kind in range(2):
            piece = jnp.dot(
                side_ref[kind, : 2 * high_rows], table_ref[row, kind, 0], preferred_element_type=jnp.float32
            )
            rest = jnp.dot(side_ref[kind, :high_rows], table_ref[row, kind, 1], preferred_element_type=jnp.float32)
            sums.append(piece[:high_rows] + piece[high_rows:] + rest)
        for index in range(count):
            block = first_block + index
            even = sums[0][index * fields : (index + 1) * fields]
            odd = sums[1][index * fields : (index + 1) * fields]
            first = pl.multiple_of(block * SPAN, SPAN)
            below = even + odd
            parts = [below[:, p * 128 : (p + 1) * 128] for p in range(HALF // 128)]
            parts = [jnp.take_along_axis(part, reverse, axis=1) for part in parts[::-1]]
            below = jnp.concatenate(parts, axis=1)
            columns = lax.broadcasted_iota(jnp.int32, (fields, HALF), 1) + first
            result_ref[row, :, pl.ds(first, HALF)] = jnp.where(columns < length, below, 0.0)
            later = pl.multiple_of(first + HALF, HALF)
            result_ref[row, :, pl.ds(later, HALF)] = jnp.where(columns + HALF < length, even - odd, 0.0)

            @pl.when(block < WHOLE)
            def _():
                send(row, block).start()

    length_fetch.wait()
    for row in range(local_rows):
        length = length_ref[row]
        block_count = (length + SPAN - 1) // SPAN
        tail = lax.rem(block_count, GROUP) == 1
        group_count = jnp.where(tail, block_count // GROUP, (block_count + GROUP - 1) // GROUP)
        filled = jnp.minimum(group_count * GROUP + tail.astype(jnp.int32), WHOLE)

        def send_empty(block, carry):
            send(row, block).start()
            return carry

        lax.fori_loop(filled, WHOLE, send_empty, 0)
        if row == 0:
            for each in range(local_rows):
                fetch_moved[each].wait()
                turn_row(each)
        fetch_turns[row].wait()
        fetch_table[row].wait()
        if row + 1 < local_rows:
            fetch_row(row + 1)

        def one_group(group, carry):
            rotate(row, group * GROUP, GROUP)

            transform(row, length, group * GROUP, GROUP)
            return carry

        lax.fori_loop(0, group_count, one_group, 0)

        @pl.when(tail)
        def _():
            rotate(row, group_count * GROUP, 1)

            transform(row, length, group_count * GROUP, 1)

        send_last(row).start()

    for row in range(local_rows):
        for block in range(WHOLE):
            send(row, block).wait()
        send_last(row).wait()


def fourier_stage(moved, tables, turns, row_longitudes):
    senders, local_rows, slots, channels = moved.shape
    total_waves = senders * slots
    fields = channels // 2
    return pl.pallas_call(
        fourier_kernel,
        in_specs=[
            pl.BlockSpec(memory_space=pl.ANY),
            pl.BlockSpec(memory_space=pl.ANY),
            pl.BlockSpec(memory_space=pltpu.HBM),
            pl.BlockSpec(memory_space=pltpu.HBM),
        ],
        out_specs=pl.BlockSpec(memory_space=pltpu.HBM),
        out_shape=jax.ShapeDtypeStruct((local_rows, fields, NLON), jnp.float32),
        scratch_shapes=[
            pltpu.SMEM(row_longitudes.shape, row_longitudes.dtype),
            pltpu.VMEM(moved.shape, moved.dtype),
            pltpu.VMEM(tables.shape, tables.dtype),
            pltpu.VMEM(turns.shape, turns.dtype),
            pltpu.VMEM((total_waves // 128, channels, 128), jnp.float32),
            pltpu.VMEM((local_rows, fields, total_waves), jnp.float32),
            pltpu.VMEM((local_rows, fields, total_waves), jnp.float32),
            pltpu.VMEM((2, 2 * GROUP * fields, total_waves), jnp.bfloat16),
            pltpu.VMEM((local_rows, fields, (BLOCKS + GROUP) * SPAN), jnp.float32),
            pltpu.SemaphoreType.DMA,
            pltpu.SemaphoreType.DMA((local_rows, 3)),
            pltpu.SemaphoreType.DMA((local_rows, BLOCKS)),
        ],
        compiler_params=pltpu.CompilerParams(vmem_limit_bytes=36 * MB),
        name="fourier",
    )(
        row_longitudes,
        moved,
        pltpu.with_memory_space_constraint(tables, pltpu.HBM),
        pltpu.with_memory_space_constraint(turns, pltpu.HBM),
    )


def per_device(legendre_values, spectra, wave_table, row_longitudes):
    slots = legendre_values.shape[0]
    devices = lax.axis_size("wave") * lax.axis_size("lev")
    local_rows = row_longitudes.shape[0]
    total_waves = wave_table.shape[0]
    sent = legendre_stage(legendre_values, spectra, wave_table)
    channels = sent.shape[2]
    moved = lax.all_to_all(
        sent.reshape(devices, local_rows * slots, channels), ("wave", "lev"), split_axis=0, concat_axis=0, tiled=True
    ).reshape(devices, local_rows, slots, channels)
    if slots % 8:
        moved = moved.swapaxes(0, 1).reshape(1, local_rows, devices * slots, channels)
    tables, turns = table_stage(wave_table, row_longitudes)
    return fourier_stage(moved, tables, turns, row_longitudes)


def solution(mesh):
    in_specs = (
        P(("wave", "lev"), None, None),
        P(("wave", "lev"), None, None),
        P(),
        P(("wave", "lev")),
    )
    out_specs = P(("wave", "lev"), None, None)
    return jax.shard_map(
        per_device, mesh=mesh, in_specs=in_specs, out_specs=out_specs, check_vma=False
    )
```

```python
import jax
import jax.numpy as jnp
import numpy as np
from jax import lax
from jax.experimental import pallas as pl
from jax.experimental.pallas import tpu as pltpu
from jax.sharding import PartitionSpec as P

NLON = 5376
HALF = 256
SPAN = 2 * HALF
BLOCKS = -(-NLON // SPAN)
BLOCK_ROWS = 16
WHOLE = NLON // SPAN
SKIP = 16
PART = 8
LARGE = 10
SMALL = 5
TILE = 256
MB = 1 << 20


def fit_turns(function, odd):
    grid = np.cos(np.pi * (np.arange(4000) + 0.5) / 4000) * 0.13 + 0.1301
    roots = np.sqrt(grid)
    values = function(2 * np.pi * roots)
    if odd:
        values = values / roots
    fitted = np.polynomial.chebyshev.Chebyshev.fit(grid, values, 7)
    return [float(c) for c in fitted.convert(kind=np.polynomial.Polynomial).coef]


COS_TERMS = fit_turns(np.cos, False)
SIN_TERMS = fit_turns(np.sin, True)


def horner(terms, square):
    total = jnp.full_like(square, terms[-1])
    for term in terms[-2::-1]:
        total = total * square + term
    return total


def cos_sin(product, double_length, inverse):
    whole = jnp.floor(product * inverse + 0.5)
    turns = (product - whole * double_length) * inverse
    square = turns * turns
    return horner(COS_TERMS, square), horner(SIN_TERMS, square) * turns


def split(values):
    high = values.astype(jnp.bfloat16)
    low = (values - high.astype(jnp.float32)).astype(jnp.bfloat16)
    return high, low


def legendre_kernel(
    group, wave_in_ref, legendre_ref, spectra_ref, out_ref, wave_ref, values_ref, kept_ref, sums_ref,
    wave_sem, value_sems, in_sems, out_sems,
):
    slots, latitudes, degree_count = legendre_ref.shape
    block_number = lax.axis_index("wave") * lax.axis_size("lev") + lax.axis_index("lev")
    first_slot = block_number * slots
    wave_fetch = pltpu.make_async_copy(wave_in_ref, wave_ref, wave_sem)
    wave_fetch.start()

    def fetch(slot):
        first = pl.multiple_of(wave_ref[first_slot + slot] // SKIP * SKIP, SKIP)
        rows = pl.ds(first, degree_count - first)
        return (
            pltpu.make_async_copy(spectra_ref.at[slot, rows, :], kept_ref.at[slot, rows, :], in_sems.at[slot]),
        )

    def fetch_values(step):
        part = pl.ds(pl.multiple_of(step * group, group), group)
        return pltpu.make_async_copy(legendre_ref.at[part], values_ref.at[part], value_sems.at[step])

    def start_slot(slot, carry):
        for copy in fetch(slot):
            copy.start()
        return carry

    def send(step):
        first = pl.multiple_of(step * group, group)
        return pltpu.make_async_copy(sums_ref.at[step], out_ref.at[:, pl.ds(first, group), :], out_sems.at[step])

    degrees = lax.broadcasted_iota(jnp.int16, kept_ref.shape[1:], 0)

    def group_sums(step, carry):
        for first in range(0, group, PART):
            part = range(first, min(first + PART, group))
            if first == 0:
                fetch_values(step).wait()
            for index in part:
                for copy in fetch(step * group + index):
                    copy.wait()
            for index in part:
                slot = step * group + index
                wave = wave_ref[first_slot + slot]
                kept = jnp.where(degrees >= wave.astype(jnp.int16), kept_ref[slot], jnp.bfloat16(0))
                sums_ref[step, :, index, :] = jnp.dot(
                    values_ref[slot], kept, preferred_element_type=jnp.float32
                )
        send(step).start()
        return carry

    def finish_send(step, carry):
        send(step).wait()
        return carry

    fetch_values(0).start()
    wave_fetch.wait()
    for step in range(slots // group):
        if step:
            fetch_values(step).start()
        lax.fori_loop(step * group, step * group + group, start_slot, 0)
    lax.fori_loop(0, slots // group, group_sums, 0)
    lax.fori_loop(0, slots // group, finish_send, 0)


def legendre_stage(legendre_values, spectra, wave_table):
    slots, latitudes, degree_count = legendre_values.shape
    channels = spectra.shape[2]
    group = 8 if slots % 8 == 0 else slots
    return pl.pallas_call(
        lambda *refs: legendre_kernel(group, *refs),
        in_specs=[pl.BlockSpec(memory_space=pltpu.HBM)] * 3,
        out_specs=pl.BlockSpec(memory_space=pltpu.HBM),
        out_shape=jax.ShapeDtypeStruct((latitudes, slots, channels), jnp.float32),
        scratch_shapes=[
            pltpu.SMEM(wave_table.shape, wave_table.dtype),
            pltpu.VMEM((slots, latitudes, degree_count), jnp.bfloat16),
            pltpu.VMEM((slots, degree_count, channels), jnp.bfloat16),
            pltpu.VMEM((slots // group, latitudes, group, channels), jnp.float32),
            pltpu.SemaphoreType.DMA,
            pltpu.SemaphoreType.DMA((slots // group,)),
            pltpu.SemaphoreType.DMA((slots,)),
            pltpu.SemaphoreType.DMA((slots // group,)),
        ],
        compiler_params=pltpu.CompilerParams(vmem_limit_bytes=60 * MB),
        name="legendre",
    )(wave_table, legendre_values, spectra)


def table_kernel(length_ref, inverse_ref, lane_waves_ref, row_waves_ref, table_ref, turn_ref):
    row = pl.program_id(0)
    length = length_ref[row]
    inverse = inverse_ref[row]
    double_length = (2 * length).astype(jnp.float32)
    total_waves = row_waves_ref.shape[0]
    chunk = 64

    def fill(step, carry):
        first = pl.multiple_of(step * chunk, chunk)
        waves = row_waves_ref[pl.ds(first, chunk), :]
        for part in range(HALF // 128):
            lanes = lax.broadcasted_iota(jnp.int32, (chunk, 128), 1) + part * 128
            offsets = (2 * lanes + 1).astype(jnp.float32)
            values = cos_sin(waves * offsets, double_length, inverse)
            for kind in range(2):
                high, low = split(values[kind])
                table_ref[0, kind, 0, pl.ds(first, chunk), pl.ds(part * 128, 128)] = high
                table_ref[0, kind, 1, pl.ds(first, chunk), pl.ds(part * 128, 128)] = low
        return carry

    lax.fori_loop(0, total_waves // chunk, fill, 0)
    blocks = lax.broadcasted_iota(jnp.int32, (BLOCK_ROWS, total_waves), 0)
    centres = (2 * SPAN * blocks + (SPAN - 1)).astype(jnp.float32)
    waves = lane_waves_ref[0:1, :]
    turn_cos, turn_sin = cos_sin(waves * centres, double_length, inverse)
    limit = lax.shift_right_logical(length - 1, 1).astype(jnp.float32)
    weight = jnp.where(waves > limit, 0.0, jnp.where(waves == 0.0, 1.0, 2.0))
    turn_ref[0, 0] = turn_cos * weight
    turn_ref[0, 1] = turn_sin * weight


def table_stage(wave_table, row_longitudes):
    total_waves = wave_table.shape[0]
    local_rows = row_longitudes.shape[0]
    waves = wave_table.astype(jnp.float32)
    lane_waves = jnp.broadcast_to(waves[None, :], (8, total_waves))
    row_waves = jnp.broadcast_to(waves[:, None], (total_waves, 128))
    inverse = 0.5 / row_longitudes.astype(jnp.float32)
    entries = local_rows * total_waves * HALF
    return pl.pallas_call(
        table_kernel,
        grid=(local_rows,),
        in_specs=[
            pl.BlockSpec(memory_space=pltpu.SMEM),
            pl.BlockSpec(memory_space=pltpu.SMEM),
            pl.BlockSpec((8, total_waves), lambda i: (0, 0)),
            pl.BlockSpec((total_waves, 128), lambda i: (0, 0)),
        ],
        out_specs=[
            pl.BlockSpec((1, 2, 2, total_waves, HALF), lambda i: (i, 0, 0, 0, 0)),
            pl.BlockSpec((1, 2, BLOCK_ROWS, total_waves), lambda i: (i, 0, 0, 0)),
        ],
        out_shape=[
            pltpu.HBM((local_rows, 2, 2, total_waves, HALF), jnp.bfloat16),
            pltpu.HBM((local_rows, 2, BLOCK_ROWS, total_waves), jnp.float32),
        ],
        compiler_params=pltpu.CompilerParams(vmem_limit_bytes=32 * MB),
        cost_estimate=pl.CostEstimate(flops=entries * 40, bytes_accessed=entries * 8, transcendentals=0),
        name="trig_tables",
    )(row_longitudes, inverse, lane_waves, row_waves)


def fourier_kernel(
    length_in_ref, moved_in_ref, table_in_ref, turn_in_ref, out_ref,
    length_ref, moved_ref, table_ref, turn_ref, flipped_ref, real_ref, imag_ref, side_ref, result_ref,
    length_sem, in_sems, out_sems,
):
    senders, local_rows, slots, channels = moved_ref.shape
    total_waves = senders * slots
    fields = channels // 2
    length_fetch = pltpu.make_async_copy(length_in_ref, length_ref, length_sem)
    fetch_moved = []
    for row in range(local_rows):
        fetch_moved.append(pltpu.make_async_copy(moved_in_ref.at[:, row], moved_ref.at[:, row], in_sems.at[row, 0]))

    def fetch_turns(row):
        return pltpu.make_async_copy(turn_in_ref.at[row], turn_ref.at[row], in_sems.at[row, 1])

    def fetch_table(row):
        return pltpu.make_async_copy(table_in_ref.at[row], table_ref.at[row], in_sems.at[row, 2])

    def fetch_row(row):
        fetch_turns(row).start()
        fetch_table(row).start()

    length_fetch.start()
    fetch_row(0)
    for row in range(local_rows):
        fetch_moved[row].start()

    def send(row, block):
        columns = pl.ds(pl.multiple_of(block * SPAN, SPAN), SPAN)
        return pltpu.make_async_copy(
            result_ref.at[row, :, columns], out_ref.at[row, :, columns], out_sems.at[row, block]
        )

    def send_last(row):
        columns = pl.ds(WHOLE * SPAN, NLON - WHOLE * SPAN)
        return pltpu.make_async_copy(
            result_ref.at[row, :, columns], out_ref.at[row, :, columns], out_sems.at[row, WHOLE]
        )

    def turn_row(row):
        moved = moved_ref[:, row].reshape(total_waves, channels)
        for step in range(total_waves // 128):
            lanes = slice(step * 128, (step + 1) * 128)
            flipped_ref[step] = moved[lanes].T
            real_ref[row, :, lanes] = flipped_ref[step, pl.ds(0, fields, stride=2), :]
            imag_ref[row, :, lanes] = flipped_ref[step, pl.ds(1, fields, stride=2), :]

    result_ref[...] = jnp.zeros_like(result_ref)
    reverse = 127 - lax.broadcasted_iota(jnp.int32, (fields, 128), 1)

    def rotate(row, first_block, count):
        for tile in range(total_waves // TILE):
            lanes = slice(tile * TILE, (tile + 1) * TILE)
            real = real_ref[row, :, lanes]
            imag = imag_ref[row, :, lanes]
            for index in range(count):
                turn_cos = turn_ref[row, 0, pl.ds(first_block + index, 1), lanes]
                turn_sin = turn_ref[row, 1, pl.ds(first_block + index, 1), lanes]
                sides = (real * turn_cos - imag * turn_sin, real * turn_sin + imag * turn_cos)
                for kind in range(2):
                    high, low = split(sides[kind])
                    side_ref[kind, index * fields : (index + 1) * fields, lanes] = high
                    side_ref[kind, (count + index) * fields : (count + index + 1) * fields, lanes] = low

    def transform(row, length, first_block, count):
        high_rows = count * fields
        sums = []
        for kind in range(2):
            piece = jnp.dot(
                side_ref[kind, : 2 * high_rows], table_ref[row, kind, 0], preferred_element_type=jnp.float32
            )
            rest = jnp.dot(side_ref[kind, :high_rows], table_ref[row, kind, 1], preferred_element_type=jnp.float32)
            sums.append(piece[:high_rows] + piece[high_rows:] + rest)
        for index in range(count):
            block = first_block + index
            even = sums[0][index * fields : (index + 1) * fields]
            odd = sums[1][index * fields : (index + 1) * fields]
            first = pl.multiple_of(block * SPAN, SPAN)
            below = even + odd
            parts = [below[:, p * 128 : (p + 1) * 128] for p in range(HALF // 128)]
            parts = [jnp.take_along_axis(part, reverse, axis=1) for part in parts[::-1]]
            below = jnp.concatenate(parts, axis=1)
            columns = lax.broadcasted_iota(jnp.int32, (fields, HALF), 1) + first
            result_ref[row, :, pl.ds(first, HALF)] = jnp.where(columns < length, below, 0.0)
            later = pl.multiple_of(first + HALF, HALF)
            result_ref[row, :, pl.ds(later, HALF)] = jnp.where(columns + HALF < length, even - odd, 0.0)

            @pl.when(block < WHOLE)
            def _():
                send(row, block).start()

    length_fetch.wait()
    for row in range(local_rows):
        fetch_moved[row].wait()
        turn_row(row)

    def one_row(row, carry):
        length = length_ref[row]
        block_count = (length + SPAN - 1) // SPAN
        large = block_count // LARGE
        rest = block_count - large * LARGE
        large = jnp.where(rest > SMALL + 1, large + 1, large)
        rest = jnp.where(rest > SMALL + 1, 0, rest)
        small = jnp.where(rest > 1, 1, 0)
        single = jnp.where((rest == 1) | (rest > SMALL), 1, 0)
        filled = large * LARGE + small * SMALL + single

        def send_empty(block, carry):
            send(row, block).start()
            return carry

        lax.fori_loop(jnp.minimum(filled, WHOLE), WHOLE, send_empty, 0)
        fetch_turns(row).wait()
        fetch_table(row).wait()

        @pl.when(row + 1 < local_rows)
        def _():
            fetch_row(row + 1)

        def groups(first_block, count, size):
            def one_group(group, carry):
                rotate(row, first_block + group * size, size)
                transform(row, length, first_block + group * size, size)
                return carry

            lax.fori_loop(0, count, one_group, 0)

        groups(0, large, LARGE)
        groups(large * LARGE, small, SMALL)
        groups(large * LARGE + small * SMALL, single, 1)
        send_last(row).start()
        return carry

    lax.fori_loop(0, local_rows, one_row, 0)
    for row in range(local_rows):
        for block in range(WHOLE):
            send(row, block).wait()
        send_last(row).wait()


def fourier_stage(moved, tables, turns, row_longitudes):
    senders, local_rows, slots, channels = moved.shape
    total_waves = senders * slots
    fields = channels // 2
    return pl.pallas_call(
        fourier_kernel,
        in_specs=[
            pl.BlockSpec(memory_space=pl.ANY),
            pl.BlockSpec(memory_space=pl.ANY),
            pl.BlockSpec(memory_space=pltpu.HBM),
            pl.BlockSpec(memory_space=pltpu.HBM),
        ],
        out_specs=pl.BlockSpec(memory_space=pltpu.HBM),
        out_shape=jax.ShapeDtypeStruct((local_rows, fields, NLON), jnp.float32),
        scratch_shapes=[
            pltpu.SMEM(row_longitudes.shape, row_longitudes.dtype),
            pltpu.VMEM(moved.shape, moved.dtype),
            pltpu.VMEM(tables.shape, tables.dtype),
            pltpu.VMEM(turns.shape, turns.dtype),
            pltpu.VMEM((total_waves // 128, channels, 128), jnp.float32),
            pltpu.VMEM((local_rows, fields, total_waves), jnp.float32),
            pltpu.VMEM((local_rows, fields, total_waves), jnp.float32),
            pltpu.VMEM((2, 2 * LARGE * fields, total_waves), jnp.bfloat16),
            pltpu.VMEM((local_rows, fields, (BLOCKS + LARGE) * SPAN), jnp.float32),
            pltpu.SemaphoreType.DMA,
            pltpu.SemaphoreType.DMA((local_rows, 3)),
            pltpu.SemaphoreType.DMA((local_rows, BLOCKS)),
        ],
        compiler_params=pltpu.CompilerParams(vmem_limit_bytes=36 * MB),
        name="fourier",
    )(
        row_longitudes,
        moved,
        pltpu.with_memory_space_constraint(tables, pltpu.HBM),
        pltpu.with_memory_space_constraint(turns, pltpu.HBM),
    )


def per_device(legendre_values, spectra, wave_table, row_longitudes):
    slots = legendre_values.shape[0]
    devices = lax.axis_size("wave") * lax.axis_size("lev")
    local_rows = row_longitudes.shape[0]
    total_waves = wave_table.shape[0]
    sent = legendre_stage(legendre_values, spectra, wave_table)
    channels = sent.shape[2]
    moved = lax.all_to_all(
        sent.reshape(devices, local_rows * slots, channels), ("wave", "lev"), split_axis=0, concat_axis=0, tiled=True
    ).reshape(devices, local_rows, slots, channels)
    if slots % 8:
        moved = moved.swapaxes(0, 1).reshape(1, local_rows, devices * slots, channels)
    tables, turns = table_stage(wave_table, row_longitudes)
    return fourier_stage(moved, tables, turns, row_longitudes)


def solution(mesh):
    in_specs = (
        P(("wave", "lev"), None, None),
        P(("wave", "lev"), None, None),
        P(),
        P(("wave", "lev")),
    )
    out_specs = P(("wave", "lev"), None, None)
    return jax.shard_map(
        per_device, mesh=mesh, in_specs=in_specs, out_specs=out_specs, check_vma=False
    )
```

```python
import jax
import jax.numpy as jnp
import numpy as np
from jax import lax
from jax.experimental import pallas as pl
from jax.experimental.pallas import tpu as pltpu
from jax.sharding import PartitionSpec as P

NLON = 5376
HALF = 256
SPAN = 2 * HALF
BLOCKS = -(-NLON // SPAN)
BLOCK_ROWS = 16
WHOLE = NLON // SPAN
SKIP = 16
PART = 8
LARGE = 10
SMALL = 5
TILE = 256
MB = 1 << 20


def fit_turns(function, odd):
    grid = np.cos(np.pi * (np.arange(4000) + 0.5) / 4000) * 0.13 + 0.1301
    roots = np.sqrt(grid)
    values = function(2 * np.pi * roots)
    if odd:
        values = values / roots
    fitted = np.polynomial.chebyshev.Chebyshev.fit(grid, values, 7)
    return [float(c) for c in fitted.convert(kind=np.polynomial.Polynomial).coef]


COS_TERMS = fit_turns(np.cos, False)
SIN_TERMS = fit_turns(np.sin, True)


def horner(terms, square):
    total = jnp.full_like(square, terms[-1])
    for term in terms[-2::-1]:
        total = total * square + term
    return total


def cos_sin(product, double_length, inverse):
    whole = jnp.floor(product * inverse + 0.5)
    turns = (product - whole * double_length) * inverse
    square = turns * turns
    return horner(COS_TERMS, square), horner(SIN_TERMS, square) * turns


def split(values):
    high = values.astype(jnp.bfloat16)
    low = (values - high.astype(jnp.float32)).astype(jnp.bfloat16)
    return high, low


def legendre_kernel(
    group, wave_in_ref, legendre_ref, spectra_ref, out_ref, wave_ref, values_ref, kept_ref, sums_ref,
    wave_sem, value_sems, in_sems, out_sems,
):
    slots, latitudes, degree_count = legendre_ref.shape
    block_number = lax.axis_index("wave") * lax.axis_size("lev") + lax.axis_index("lev")
    first_slot = block_number * slots
    wave_fetch = pltpu.make_async_copy(wave_in_ref, wave_ref, wave_sem)
    wave_fetch.start()

    def fetch(slot):
        first = pl.multiple_of(wave_ref[first_slot + slot] // SKIP * SKIP, SKIP)
        rows = pl.ds(first, degree_count - first)
        return (
            pltpu.make_async_copy(spectra_ref.at[slot, rows, :], kept_ref.at[slot, rows, :], in_sems.at[slot]),
        )

    def fetch_values(step):
        part = pl.ds(pl.multiple_of(step * group, group), group)
        return pltpu.make_async_copy(legendre_ref.at[part], values_ref.at[part], value_sems.at[step])

    def start_slot(slot, carry):
        for copy in fetch(slot):
            copy.start()
        return carry

    def send(step):
        first = pl.multiple_of(step * group, group)
        return pltpu.make_async_copy(sums_ref.at[step], out_ref.at[:, pl.ds(first, group), :], out_sems.at[step])

    degrees = lax.broadcasted_iota(jnp.int16, kept_ref.shape[1:], 0)

    def group_sums(step, carry):
        for first in range(0, group, PART):
            part = range(first, min(first + PART, group))
            if first == 0:
                fetch_values(step).wait()
            for index in part:
                for copy in fetch(step * group + index):
                    copy.wait()
            for index in part:
                slot = step * group + index
                wave = wave_ref[first_slot + slot]
                kept = jnp.where(degrees >= wave.astype(jnp.int16), kept_ref[slot], jnp.bfloat16(0))
                sums_ref[step, :, index, :] = jnp.dot(
                    values_ref[slot], kept, preferred_element_type=jnp.float32
                )
        send(step).start()
        return carry

    def finish_send(step, carry):
        send(step).wait()
        return carry

    fetch_values(0).start()
    wave_fetch.wait()
    for step in range(slots // group):
        if step:
            fetch_values(step).start()
        lax.fori_loop(step * group, step * group + group, start_slot, 0)
    lax.fori_loop(0, slots // group, group_sums, 0)
    lax.fori_loop(0, slots // group, finish_send, 0)


def legendre_stage(legendre_values, spectra, wave_table):
    slots, latitudes, degree_count = legendre_values.shape
    channels = spectra.shape[2]
    group = 8 if slots % 8 == 0 else slots
    return pl.pallas_call(
        lambda *refs: legendre_kernel(group, *refs),
        in_specs=[pl.BlockSpec(memory_space=pltpu.HBM)] * 3,
        out_specs=pl.BlockSpec(memory_space=pltpu.HBM),
        out_shape=jax.ShapeDtypeStruct((latitudes, slots, channels), jnp.float32),
        scratch_shapes=[
            pltpu.SMEM(wave_table.shape, wave_table.dtype),
            pltpu.VMEM((slots, latitudes, degree_count), jnp.bfloat16),
            pltpu.VMEM((slots, degree_count, channels), jnp.bfloat16),
            pltpu.VMEM((slots // group, latitudes, group, channels), jnp.float32),
            pltpu.SemaphoreType.DMA,
            pltpu.SemaphoreType.DMA((slots // group,)),
            pltpu.SemaphoreType.DMA((slots,)),
            pltpu.SemaphoreType.DMA((slots // group,)),
        ],
        compiler_params=pltpu.CompilerParams(vmem_limit_bytes=60 * MB),
        name="legendre",
    )(wave_table, legendre_values, spectra)


def table_kernel(length_ref, inverse_ref, lane_waves_ref, row_waves_ref, table_ref, turn_ref):
    row = pl.program_id(0)
    length = length_ref[row]
    inverse = inverse_ref[row]
    double_length = (2 * length).astype(jnp.float32)
    total_waves = row_waves_ref.shape[0]
    chunk = 64

    def fill(step, carry):
        first = pl.multiple_of(step * chunk, chunk)
        waves = row_waves_ref[pl.ds(first, chunk), :]
        for part in range(HALF // 128):
            lanes = lax.broadcasted_iota(jnp.int32, (chunk, 128), 1) + part * 128
            offsets = (2 * lanes + 1).astype(jnp.float32)
            values = cos_sin(waves * offsets, double_length, inverse)
            for kind in range(2):
                high, low = split(values[kind])
                table_ref[0, kind, 0, pl.ds(first, chunk), pl.ds(part * 128, 128)] = high
                table_ref[0, kind, 1, pl.ds(first, chunk), pl.ds(part * 128, 128)] = low
        return carry

    lax.fori_loop(0, total_waves // chunk, fill, 0)
    blocks = lax.broadcasted_iota(jnp.int32, (BLOCK_ROWS, total_waves), 0)
    centres = (2 * SPAN * blocks + (SPAN - 1)).astype(jnp.float32)
    waves = lane_waves_ref[0:1, :]
    turn_cos, turn_sin = cos_sin(waves * centres, double_length, inverse)
    limit = lax.shift_right_logical(length - 1, 1).astype(jnp.float32)
    weight = jnp.where(waves > limit, 0.0, jnp.where(waves == 0.0, 1.0, 2.0))
    turn_ref[0, 0] = turn_cos * weight
    turn_ref[0, 1] = turn_sin * weight


def table_stage(wave_table, row_longitudes):
    total_waves = wave_table.shape[0]
    local_rows = row_longitudes.shape[0]
    waves = wave_table.astype(jnp.float32)
    lane_waves = jnp.broadcast_to(waves[None, :], (8, total_waves))
    row_waves = jnp.broadcast_to(waves[:, None], (total_waves, 128))
    inverse = 0.5 / row_longitudes.astype(jnp.float32)
    entries = local_rows * total_waves * HALF
    return pl.pallas_call(
        table_kernel,
        grid=(local_rows,),
        in_specs=[
            pl.BlockSpec(memory_space=pltpu.SMEM),
            pl.BlockSpec(memory_space=pltpu.SMEM),
            pl.BlockSpec((8, total_waves), lambda i: (0, 0)),
            pl.BlockSpec((total_waves, 128), lambda i: (0, 0)),
        ],
        out_specs=[
            pl.BlockSpec((1, 2, 2, total_waves, HALF), lambda i: (i, 0, 0, 0, 0)),
            pl.BlockSpec((1, 2, BLOCK_ROWS, total_waves), lambda i: (i, 0, 0, 0)),
        ],
        out_shape=[
            pltpu.HBM((local_rows, 2, 2, total_waves, HALF), jnp.bfloat16),
            pltpu.HBM((local_rows, 2, BLOCK_ROWS, total_waves), jnp.float32),
        ],
        compiler_params=pltpu.CompilerParams(vmem_limit_bytes=32 * MB),
        cost_estimate=pl.CostEstimate(flops=entries * 40, bytes_accessed=entries * 8, transcendentals=0),
        name="trig_tables",
    )(row_longitudes, inverse, lane_waves, row_waves)


def fourier_kernel(
    length_in_ref, moved_in_ref, table_in_ref, turn_in_ref, out_ref,
    length_ref, moved_ref, table_ref, turn_ref, flipped_ref, real_ref, imag_ref, side_ref, result_ref,
    length_sem, in_sems, out_sems,
):
    senders, local_rows, slots, channels = moved_ref.shape
    total_waves = senders * slots
    fields = channels // 2
    length_fetch = pltpu.make_async_copy(length_in_ref, length_ref, length_sem)
    fetch_moved = []
    for row in range(local_rows):
        fetch_moved.append(pltpu.make_async_copy(moved_in_ref.at[:, row], moved_ref.at[:, row], in_sems.at[row, 0]))

    def fetch_turns(row):
        return pltpu.make_async_copy(turn_in_ref.at[row], turn_ref.at[row], in_sems.at[row, 1])

    def fetch_table(row):
        return pltpu.make_async_copy(table_in_ref.at[row], table_ref.at[row], in_sems.at[row, 2])

    def fetch_row(row):
        fetch_turns(row).start()
        fetch_table(row).start(priority=1)

    length_fetch.start()
    fetch_row(0)
    for row in range(local_rows):
        fetch_moved[row].start()

    def send(row, block):
        columns = pl.ds(pl.multiple_of(block * SPAN, SPAN), SPAN)
        return pltpu.make_async_copy(
            result_ref.at[row, :, columns], out_ref.at[row, :, columns], out_sems.at[row, block]
        )

    def send_last(row):
        columns = pl.ds(WHOLE * SPAN, NLON - WHOLE * SPAN)
        return pltpu.make_async_copy(
            result_ref.at[row, :, columns], out_ref.at[row, :, columns], out_sems.at[row, WHOLE]
        )

    def turn_row(row):
        moved = moved_ref[:, row].reshape(total_waves, channels)
        for step in range(total_waves // 128):
            lanes = slice(step * 128, (step + 1) * 128)
            flipped_ref[step] = moved[lanes].T
            real_ref[row, :, lanes] = flipped_ref[step, pl.ds(0, fields, stride=2), :]
            imag_ref[row, :, lanes] = flipped_ref[step, pl.ds(1, fields, stride=2), :]

    result_ref[...] = jnp.zeros_like(result_ref)
    reverse = 127 - lax.broadcasted_iota(jnp.int32, (fields, 128), 1)

    def rotate(row, first_block, count):
        for tile in range(total_waves // TILE):
            lanes = slice(tile * TILE, (tile + 1) * TILE)
            real = real_ref[row, :, lanes]
            imag = imag_ref[row, :, lanes]
            for index in range(count):
                turn_cos = turn_ref[row, 0, pl.ds(first_block + index, 1), lanes]
                turn_sin = turn_ref[row, 1, pl.ds(first_block + index, 1), lanes]
                sides = (real * turn_cos - imag * turn_sin, real * turn_sin + imag * turn_cos)
                for kind in range(2):
                    high, low = split(sides[kind])
                    side_ref[kind, index * fields : (index + 1) * fields, lanes] = high
                    side_ref[kind, (count + index) * fields : (count + index + 1) * fields, lanes] = low

    def transform(row, length, first_block, count):
        high_rows = count * fields
        sums = []
        for kind in range(2):
            piece = jnp.dot(
                side_ref[kind, : 2 * high_rows], table_ref[row, kind, 0], preferred_element_type=jnp.float32
            )
            rest = jnp.dot(side_ref[kind, :high_rows], table_ref[row, kind, 1], preferred_element_type=jnp.float32)
            sums.append(piece[:high_rows] + piece[high_rows:] + rest)
        for index in range(count):
            block = first_block + index
            even = sums[0][index * fields : (index + 1) * fields]
            odd = sums[1][index * fields : (index + 1) * fields]
            first = pl.multiple_of(block * SPAN, SPAN)
            below = even + odd
            parts = [below[:, p * 128 : (p + 1) * 128] for p in range(HALF // 128)]
            parts = [jnp.take_along_axis(part, reverse, axis=1) for part in parts[::-1]]
            below = jnp.concatenate(parts, axis=1)
            columns = lax.broadcasted_iota(jnp.int32, (fields, HALF), 1) + first
            result_ref[row, :, pl.ds(first, HALF)] = jnp.where(columns < length, below, 0.0)
            later = pl.multiple_of(first + HALF, HALF)
            result_ref[row, :, pl.ds(later, HALF)] = jnp.where(columns + HALF < length, even - odd, 0.0)

            @pl.when(block < WHOLE)
            def _():
                send(row, block).start()

    length_fetch.wait()
    for row in range(local_rows):
        fetch_moved[row].wait()
        turn_row(row)

    def one_row(row, carry):
        length = length_ref[row]
        block_count = (length + SPAN - 1) // SPAN
        large = block_count // LARGE
        rest = block_count - large * LARGE
        large = jnp.where(rest > SMALL + 1, large + 1, large)
        rest = jnp.where(rest > SMALL + 1, 0, rest)
        small = jnp.where(rest > 1, 1, 0)
        single = jnp.where((rest == 1) | (rest > SMALL), 1, 0)
        filled = large * LARGE + small * SMALL + single

        def send_empty(block, carry):
            send(row, block).start()
            return carry

        lax.fori_loop(jnp.minimum(filled, WHOLE), WHOLE, send_empty, 0)
        fetch_turns(row).wait()
        fetch_table(row).wait()

        @pl.when(row + 1 < local_rows)
        def _():
            fetch_row(row + 1)

        def groups(first_block, count, size):
            def one_group(group, carry):
                rotate(row, first_block + group * size, size)
                transform(row, length, first_block + group * size, size)
                return carry

            lax.fori_loop(0, count, one_group, 0)

        groups(0, large, LARGE)
        groups(large * LARGE, small, SMALL)
        groups(large * LARGE + small * SMALL, single, 1)
        send_last(row).start()
        return carry

    lax.fori_loop(0, local_rows, one_row, 0)
    for row in range(local_rows):
        for block in range(WHOLE):
            send(row, block).wait()
        send_last(row).wait()


def fourier_stage(moved, tables, turns, row_longitudes):
    senders, local_rows, slots, channels = moved.shape
    total_waves = senders * slots
    fields = channels // 2
    return pl.pallas_call(
        fourier_kernel,
        in_specs=[
            pl.BlockSpec(memory_space=pl.ANY),
            pl.BlockSpec(memory_space=pl.ANY),
            pl.BlockSpec(memory_space=pltpu.HBM),
            pl.BlockSpec(memory_space=pltpu.HBM),
        ],
        out_specs=pl.BlockSpec(memory_space=pltpu.HBM),
        out_shape=jax.ShapeDtypeStruct((local_rows, fields, NLON), jnp.float32),
        scratch_shapes=[
            pltpu.SMEM(row_longitudes.shape, row_longitudes.dtype),
            pltpu.VMEM(moved.shape, moved.dtype),
            pltpu.VMEM(tables.shape, tables.dtype),
            pltpu.VMEM(turns.shape, turns.dtype),
            pltpu.VMEM((total_waves // 128, channels, 128), jnp.float32),
            pltpu.VMEM((local_rows, fields, total_waves), jnp.float32),
            pltpu.VMEM((local_rows, fields, total_waves), jnp.float32),
            pltpu.VMEM((2, 2 * LARGE * fields, total_waves), jnp.bfloat16),
            pltpu.VMEM((local_rows, fields, (BLOCKS + LARGE) * SPAN), jnp.float32),
            pltpu.SemaphoreType.DMA,
            pltpu.SemaphoreType.DMA((local_rows, 3)),
            pltpu.SemaphoreType.DMA((local_rows, BLOCKS)),
        ],
        compiler_params=pltpu.CompilerParams(vmem_limit_bytes=36 * MB),
        name="fourier",
    )(
        row_longitudes,
        moved,
        pltpu.with_memory_space_constraint(tables, pltpu.HBM),
        pltpu.with_memory_space_constraint(turns, pltpu.HBM),
    )


def per_device(legendre_values, spectra, wave_table, row_longitudes):
    slots = legendre_values.shape[0]
    devices = lax.axis_size("wave") * lax.axis_size("lev")
    local_rows = row_longitudes.shape[0]
    total_waves = wave_table.shape[0]
    sent = legendre_stage(legendre_values, spectra, wave_table)
    channels = sent.shape[2]
    moved = lax.all_to_all(
        sent.reshape(devices, local_rows * slots, channels), ("wave", "lev"), split_axis=0, concat_axis=0, tiled=True
    ).reshape(devices, local_rows, slots, channels)
    if slots % 8:
        moved = moved.swapaxes(0, 1).reshape(1, local_rows, devices * slots, channels)
    tables, turns = table_stage(wave_table, row_longitudes)
    return fourier_stage(moved, tables, turns, row_longitudes)


def solution(mesh):
    in_specs = (
        P(("wave", "lev"), None, None),
        P(("wave", "lev"), None, None),
        P(),
        P(("wave", "lev")),
    )
    out_specs = P(("wave", "lev"), None, None)
    return jax.shard_map(
        per_device, mesh=mesh, in_specs=in_specs, out_specs=out_specs, check_vma=False
    )
```
